256 devices in a mesh: row: 4 (over z_hi), col: 8 (over y, core), depth: 8 (over z_lo, x).
Axes of the slice: x: 4, y: 4, z: 8 (z_hi: 4, z_lo: 2; z = z_hi * 2 + z_lo), core: 2. Of those that a mesh axis runs over, the one named last changes fastest.
Arguments:
- grad_out: bfloat16 [8, 2048, 8192], P('depth', 'col', 'row'), may hold values from -0.046875 to 0.046875
- inputs: bfloat16 [8, 2048, 8192], P('depth', 'row', 'col'), may hold values from -6 to 6
Outputs:
- grad_weight: bfloat16 [8192, 8192], P(('row', 'depth'), 'col')
The draws below stay inside these ranges and needn't reach their ends.
All inputs are finite; a program needn't handle non-finite values.
Results may differ from the reference program's by a relative error of at most 0.001.
Values may be sent and summed in bfloat16 or wider, within the bound.
No kernel may reach another device: no remote copies, remote signals or barrier semaphores. Data moves between devices by JAX's collectives and lax.ppermute only.
A program may use at most 64 MiB of HBM per device.

```python
import jax
import jax.numpy as jnp

D = 8192
LAYER_TOK = 2048
MICRO = 8
TOKENS = 16384


def strengthened(array, stream_key, source, target, parts, factor):
    owner, partner = [(jnp.arange(array.shape[dim]) // (array.shape[dim] // parts)).reshape([-1 if axis == dim else 1 for axis in range(array.ndim)]) for dim in (source, target)]
    chosen = jax.random.permutation(stream_key, parts)[partner]
    strong = (owner == chosen) | (owner == (partner + parts // 2) % parts)
    return jnp.where(strong, factor * array, array)


def block_scale(stream_key, dims, split, smallest, largest):
    gain, own = 1.0, jax.random.fold_in(stream_key, 6)
    for axis_at, blocks in split:
        steps = jnp.exp(jax.random.uniform(jax.random.fold_in(own, axis_at), (blocks,), jnp.float32, smallest / len(split), largest / len(split)))
        gain = gain * jnp.repeat(steps, dims[axis_at] // blocks).reshape([-1 if axis == axis_at else 1 for axis in range(len(dims))])
    return gain


def scatter_about(stream_key, extent, deviation, limit, shards=(), dtype=jnp.bfloat16):
    entries = jax.random.normal(stream_key, extent, jnp.float32) * deviation
    if len(shards) > 0:
        entries = block_scale(stream_key, extent, shards, -0.22, 0.18) * entries
    return jnp.clip(entries, min=-limit, max=limit).astype(dtype)


def gaussian_with(own_key, extent, scale, limit, pieces, heavy, dtype=jnp.bfloat16):
    drawn = scale * jax.random.normal(own_key, extent, jnp.float32)
    if pieces:
        drawn = drawn * block_scale(own_key, extent, pieces, -0.22, 0.18)
    return jnp.clip(strengthened(drawn, jax.random.fold_in(own_key, 3), *heavy), -limit, limit).astype(dtype)


def setup_inputs(seed: int = 0) -> dict:
    key_of = jax.random.split(jax.random.key(seed), 3)
    return {
        "grad_out": gaussian_with(key_of[0], (MICRO, LAYER_TOK, D), (1.0 / TOKENS ** 0.5), 0.046875, ((0, 8), (1, 8), (2, 4)), (0, 2, 8, 2.0)),
        "inputs": scatter_about(key_of[1], (MICRO, LAYER_TOK, D), 1.0, 6.0, ((0, 8), (1, 4), (2, 8))),
    }


def reference(grad_out, inputs):
    width = grad_out.shape[2]
    left = grad_out.reshape(-1, width)
    right = inputs.reshape(-1, width)
    result = jnp.dot(left.T, right, preferred_element_type=jnp.float32)
    return result.astype(jnp.bfloat16)
```

```python
import jax
import jax.numpy as jnp
from jax import lax
from jax.sharding import Mesh, PartitionSpec as P

Z = ("zh", "zl")
CHUNKS = (512, 512)


def shifted(x, axis, n, step):
    return lax.ppermute(x, axis, [(i, (i + step) % n) for i in range(n)])


def tokens_dot(g, x):
    return lax.dot_general(g, x, (((0,), (0,)), ((), ())), preferred_element_type=jnp.float32)


def gathered_along_z(x):
    up, down = {0: x}, {0: x}
    for s in range(1, 4):
        up[s] = shifted(up[s - 1], Z, 8, 1)
        down[s] = shifted(down[s - 1], Z, 8, -1)
    half = x.shape[0] // 2
    far = (shifted(up[3][:half], Z, 8, 1), shifted(down[3][half:], Z, 8, -1))
    return up, down, far


def summed_over_x(total):
    x = lax.axis_index("x")
    rows, width = total.shape[0] // 4, total.shape[1]
    block = lambda d: lax.dynamic_slice_in_dim(total, (x + d) % 4 * rows, rows, 0)
    half = width // 2
    far = block(2)
    left = shifted(far[:, :half], "x", 4, 1)
    right = shifted(far[:, half:], "x", 4, -1)
    ahead, behind = block(1), block(3)
    ahead = jnp.concatenate([ahead[:, :half] + left, ahead[:, half:]], 1)
    behind = jnp.concatenate([behind[:, :half], behind[:, half:] + right], 1)
    return block(0) + shifted(ahead, "x", 4, 1) + shifted(behind, "x", 4, -1)


def body(grad_out, inputs):
    g, x = grad_out[0], inputs[0]
    zh, zl = lax.axis_index("zh"), lax.axis_index("zl")
    z = zh * 2 + zl
    rows = g.shape[1] // 2
    mine = lax.dynamic_slice_in_dim(g, zl * rows, rows, 1)
    other = lax.dynamic_slice_in_dim(g, (1 - zl) * rows, rows, 1)
    even = lax.all_gather(mine, ("y", "c"), axis=0, tiled=True)
    odd = lax.all_gather(lax.ppermute(other, "zl", [(0, 1), (1, 0)]), ("y", "c"), axis=0, tiled=True)
    tok = x.shape[0]

    def g_of(s, start=0, size=tok):
        owner = (z - s + 8) % 8 // 2
        return lax.dynamic_slice_in_dim(odd if s % 2 else even, owner * tok + start, size, 0)

    outs, at = [], 0
    for width in CHUNKS:
        up, down, far = gathered_along_z(x[:, at : at + width])
        at += width
        total = tokens_dot(g_of(0), up[0])
        for s in range(1, 4):
            total += tokens_dot(g_of(s), up[s])
            total += tokens_dot(g_of(-s), down[s])
        half = tok // 2
        total += tokens_dot(g_of(4, 0, half), far[0])
        total += tokens_dot(g_of(4, half, half), far[1])
        outs.append(summed_over_x(total).astype(jnp.bfloat16))
    return jnp.concatenate(outs, 1)


def solution(mesh):
    devices = mesh.devices.reshape(4, 4, 2, 2, 4)
    return jax.shard_map(
        body,
        mesh=Mesh(devices, ("zh", "y", "c", "zl", "x")),
        in_specs=(P(("zl", "x"), ("y", "c"), "zh"), P(("zl", "x"), "zh", ("y", "c"))),
        out_specs=P(("zh", "zl", "x"), ("y", "c")),
        check_vma=False,
    )
```

```python
import jax
import jax.numpy as jnp
from jax import lax
from jax.experimental import pallas as pl
from jax.experimental.pallas import tpu as pltpu
from jax.sharding import Mesh, PartitionSpec as P

FIRST = 640


def after(x, *earlier):
    return lax.optimization_barrier((x, *earlier))[0]


def along(x, axis, way):
    inner = axis == "x"
    at = lambda i, c: c * 4 + i if inner else i * 2 + c
    pairs = [(at(i, c), at((i + (way if c == 0 else -way)) % 4, c)) for i in range(4) for c in range(2)]
    return lax.ppermute(x, ("c", "x") if inner else ("y", "c"), pairs)


def opposite(x, axis):
    return lax.ppermute(x, axis, [(i, (i + 2) % 4) for i in range(4)])


def other_core(x):
    return lax.ppermute(x, "c", [(0, 1), (1, 0)])


def product_kernel(where, *refs):
    grads, (x_ref, out_ref) = refs[:16], refs[16:]
    half = grads[0].shape[0]
    total = None
    for shard in range(8):
        for held in range(2):
            core = where[3 * 8] if held == 0 else 1 - where[3 * 8]
            start = pl.multiple_of(shard * 2 * half + core * half, half)
            term = lax.dot_general(
                grads[shard * 2 + held][...],
                x_ref[pl.ds(start, half), :],
                (((0,), (0,)), ((), ())),
                preferred_element_type=jnp.float32,
            )
            total = term if total is None else total + term
    out_ref[...] = total


def product(where, own, theirs, x):
    _, _, half, rows = own.shape
    width, step = x.shape[1], 256

    def block(shard, held):
        def index(f, where):
            return where[3 * shard + held], where[3 * shard + 2], 0, f

        return pl.BlockSpec((None, None, half, step), index)

    specs = [block(shard, held) for shard in range(8) for held in range(2)]
    return pl.pallas_call(
        product_kernel,
        grid_spec=pltpu.PrefetchScalarGridSpec(
            num_scalar_prefetch=1,
            grid=(rows // step,),
            in_specs=[*specs, pl.BlockSpec(x.shape, lambda f, where: (0, 0))],
            out_specs=pl.BlockSpec((step, width), lambda f, where: (f, 0)),
        ),
        out_shape=jax.ShapeDtypeStruct((rows, width), jnp.float32),
        compiler_params=pltpu.CompilerParams(vmem_limit_bytes=40 * 2**20),
        cost_estimate=pl.CostEstimate(
            flops=2 * x.size * rows,
            bytes_accessed=4 * own.size + 2 * x.size + 4 * rows * width,
            transcendentals=0,
        ),
    )(where, *([own, theirs] * 8), x)


def body(grad_out, inputs):
    g, x = grad_out[0], inputs[0]
    zh, zl, y, me, c = (lax.axis_index(name) for name in ("zh", "zl", "y", "x", "c"))
    way = 1 - 2 * c
    z = zh * 2 + zl
    rows, tok = g.shape[1] // 2, x.shape[0]
    half, block = tok // 2, rows // 4
    a = lax.all_gather(x[:, :FIRST], ("zh", "zl"), axis=0, tiled=True)
    b = lax.all_gather(after(x[:, FIRST:], a), ("zh", "zl"), axis=0, tiled=True)

    mine = lax.dynamic_slice_in_dim(g, zl * rows, rows, 1)
    swapped = lax.dynamic_slice_in_dim(g, (1 - zl) * rows, rows, 1)
    pair = jnp.stack([mine, lax.ppermute(swapped, "zl", [(0, 1), (1, 0)])])
    first, last = along(pair, "y", 1), along(pair, "y", -1)
    middle = jnp.stack([along(first[0], "y", 1), along(last[1], "y", -1)])
    own = jnp.stack([pair, first, middle, last])
    theirs = other_core(own)

    where = []
    for shard in range(8):
        index = (way * (y - shard // 2) + 8) % 4
        where += [index, (4 - index) % 4, (shard + zl) % 2]
    where = jnp.stack([*where, c]).astype(jnp.int32)

    def part(total, d):
        return lax.dynamic_slice_in_dim(total, (me + way * d + 4) % 4 * block, block, 0)

    sum_a = product(where, own, theirs, a)
    edge = block // 2
    far, ahead, behind = part(sum_a, 2), part(sum_a, 1), part(sum_a, -1)
    ahead = jnp.concatenate([ahead[:edge] + along(far[:edge], "x", 1), ahead[edge:]])
    behind = jnp.concatenate([behind[:edge], behind[edge:] + along(far[edge:], "x", -1)])
    out_a = part(sum_a, 0) + along(ahead, "x", 1) + along(behind, "x", -1)
    sum_b = product(where, own, theirs, b)
    far = opposite(part(sum_b, 2), "x")
    out_b = part(sum_b, 0) + along(part(sum_b, 1), "x", 1) + along(part(sum_b, -1), "x", -1) + far
    return jnp.concatenate([out_a, out_b], 1).astype(jnp.bfloat16)


def solution(mesh):
    devices = mesh.devices.reshape(4, 4, 2, 2, 4)
    return jax.shard_map(
        body,
        mesh=Mesh(devices, ("zh", "y", "c", "zl", "x")),
        in_specs=(P(("zl", "x"), ("y", "c"), "zh"), P(("zl", "x"), "zh", ("y", "c"))),
        out_specs=P(("zh", "zl", "x"), ("y", "c")),
        check_vma=False,
    )
```

```python
import functools

import jax
import jax.numpy as jnp
from jax import lax
from jax.experimental import pallas as pl
from jax.experimental.pallas import tpu as pltpu
from jax.sharding import Mesh, PartitionSpec as P

FIRST = 640


def along(x, axis, way):
    inner = axis == "x"
    at = lambda i, c: c * 4 + i if inner else i * 2 + c
    pairs = [(at(i, c), at((i + (way if c == 0 else -way)) % 4, c)) for i in range(4) for c in range(2)]
    return lax.ppermute(x, ("c", "x") if inner else ("y", "c"), pairs)


def opposite(x, axis):
    return lax.ppermute(x, axis, [(i, (i + 2) % 4) for i in range(4)])


def other_core(x):
    return lax.ppermute(x, "c", [(0, 1), (1, 0)])


def product_kernel(where, *refs):
    grads, x_ref, outs = refs[:16], refs[16], refs[17:]
    half = grads[0].shape[0]
    total = None
    for k, grad in enumerate(grads):
        tokens = x_ref[pl.ds(pl.multiple_of(where[16 + k], half), half), :]
        term = lax.dot_general(grad[...], tokens, (((0,), (0,)), ((), ())), preferred_element_type=jnp.float32)
        total = term if total is None else total + term
    for step, out in enumerate(outs):
        pl.when(pl.program_id(0) == step)(functools.partial(out.__setitem__, ..., total))


def product(where, own, theirs, x, blocks):
    half, rows = own.shape[2:]
    width, block = x.shape[1], rows // 4

    def grad_block(k):
        return pl.BlockSpec((None, None, half, block), lambda i, where: (where[k], k // 2 % 2, 0, where[32 + blocks[0] + i]))

    out = jax.ShapeDtypeStruct((block, width), jnp.float32)
    return pl.pallas_call(
        product_kernel,
        grid_spec=pltpu.PrefetchScalarGridSpec(
            num_scalar_prefetch=1,
            grid=(len(blocks),),
            in_specs=[*map(grad_block, range(16)), pl.BlockSpec(x.shape, lambda i, where: (0, 0))],
            out_specs=[pl.BlockSpec((block, width), lambda i, where: (0, 0))] * len(blocks),
        ),
        out_shape=[out] * len(blocks),
        compiler_params=pltpu.CompilerParams(vmem_limit_bytes=40 * 2**20),
        cost_estimate=pl.CostEstimate(
            flops=2 * x.size * block * len(blocks),
            bytes_accessed=2 * x.size + (2 * x.shape[0] + 4 * width) * block * len(blocks),
            transcendentals=0,
        ),
    )(where, *([own, theirs] * 8), x)


def body(grad_out, inputs):
    g, x = grad_out[0], inputs[0]
    zh, zl, y, me, c = (lax.axis_index(name) for name in ("zh", "zl", "y", "x", "c"))
    way = 1 - 2 * c
    z = zh * 2 + zl
    rows, tok = g.shape[1] // 2, x.shape[0]
    half, block = tok // 2, rows // 4
    mine = lax.dynamic_slice_in_dim(g, zl * rows, rows, 1)
    swapped = lax.ppermute(lax.dynamic_slice_in_dim(g, (1 - zl) * rows, rows, 1), "zl", [(0, 1), (1, 0)])
    a = lax.all_gather(x[:, :FIRST], ("zh", "zl"), axis=0, tiled=True)
    b = lax.optimization_barrier((x, swapped))[0][:, FIRST:]

    pair = jnp.stack([mine, swapped])
    first, last = along(pair, "y", 1), along(pair, "y", -1)
    middle = jnp.stack([along(first[0], "y", 1), along(last[1], "y", -1)])
    own = jnp.stack([pair, first, middle, last])
    b = lax.all_gather(lax.optimization_barrier((b, a, own))[0], ("zh", "zl"), axis=0, tiled=True)
    theirs = other_core(own)

    places, starts = [], []
    for s in range(8):
        owner = (z - s + 8) % 8
        index = (way * (y - owner // 2) + 8) % 4
        places += [index, (4 - index) % 4]
        starts += [owner * tok + c * half, owner * tok + (1 - c) * half]
    blocks = [(me + way * d + 4) % 4 for d in (2, 1, -1, 0)]
    where = jnp.stack([*places, *starts, *blocks]).astype(jnp.int32)

    def summed(x_all):
        edge = block // 2
        (far,) = product(where, own, theirs, x_all, (0,))
        up, down = along(far[:edge], "x", 1), along(far[edge:], "x", -1)
        ahead, behind = product(where, own, theirs, x_all, (1, 2))
        ahead = jnp.concatenate([ahead[:edge] + up, ahead[edge:]])
        behind = jnp.concatenate([behind[:edge], behind[edge:] + down])
        up, down = along(ahead, "x", 1), along(behind, "x", -1)
        (out,) = product(where, own, theirs, x_all, (3,))
        return (out + up + down).astype(jnp.bfloat16)

    out_a = summed(a)
    out_b = summed(lax.optimization_barrier((b, out_a))[0])
    return jnp.concatenate([out_a, out_b], 1)


def solution(mesh):
    devices = mesh.devices.reshape(4, 4, 2, 2, 4)
    return jax.shard_map(
        body,
        mesh=Mesh(devices, ("zh", "y", "c", "zl", "x")),
        in_specs=(P(("zl", "x"), ("y", "c"), "zh"), P(("zl", "x"), "zh", ("y", "c"))),
        out_specs=P(("zh", "zl", "x"), ("y", "c")),
        check_vma=False,
    )
```

```python
import functools

import jax
import jax.numpy as jnp
from jax import lax
from jax.experimental import pallas as pl
from jax.experimental.pallas import tpu as pltpu
from jax.sharding import Mesh, PartitionSpec as P

FIRST = 640


def along(x, axis, way):
    inner = axis == "x"
    at = lambda i, c: c * 4 + i if inner else i * 2 + c
    pairs = [(at(i, c), at((i + (way if c == 0 else -way)) % 4, c)) for i in range(4) for c in range(2)]
    return lax.ppermute(x, ("c", "x") if inner else ("y", "c"), pairs)


def other_core(x):
    return lax.ppermute(x, "c", [(0, 1), (1, 0)])


def product_kernel(where, *refs):
    grads, x_ref, outs = refs[:16], refs[16], refs[17:]
    half = grads[0].shape[0]
    total = None
    for k, grad in enumerate(grads):
        tokens = x_ref[pl.ds(pl.multiple_of(where[16 + k], half), half), :]
        term = lax.dot_general(grad[...], tokens, (((0,), (0,)), ((), ())), preferred_element_type=jnp.float32)
        total = term if total is None else total + term
    for step, out in enumerate(outs):
        pl.when(pl.program_id(0) == step)(functools.partial(out.__setitem__, ..., total))


def product(where, own, theirs, x, blocks):
    half, rows = own.shape[2:]
    width, block = x.shape[1], rows // 4

    def grad_block(k):
        return pl.BlockSpec((None, None, half, block), lambda i, where: (where[k], k // 2 % 2, 0, where[32 + blocks[0] + i]))

    out = jax.ShapeDtypeStruct((block, width), jnp.float32)
    return pl.pallas_call(
        product_kernel,
        grid_spec=pltpu.PrefetchScalarGridSpec(
            num_scalar_prefetch=1,
            grid=(len(blocks),),
            in_specs=[*map(grad_block, range(16)), pl.BlockSpec(x.shape, lambda i, where: (0, 0))],
            out_specs=[pl.BlockSpec((block, width), lambda i, where: (0, 0))] * len(blocks),
        ),
        out_shape=[out] * len(blocks),
        compiler_params=pltpu.CompilerParams(vmem_limit_bytes=22 * 2**20),
        cost_estimate=pl.CostEstimate(
            flops=2 * x.size * block * len(blocks),
            bytes_accessed=2 * x.size + (2 * x.shape[0] + 4 * width) * block * len(blocks),
            transcendentals=0,
        ),
    )(where, *([own, theirs] * 8), x)


def body(grad_out, inputs):
    g, x = grad_out[0], inputs[0]
    zh, zl, y, me, c = (lax.axis_index(name) for name in ("zh", "zl", "y", "x", "c"))
    way = 1 - 2 * c
    z = zh * 2 + zl
    rows, tok = g.shape[1] // 2, x.shape[0]
    half, block = tok // 2, rows // 4
    mine = lax.dynamic_slice_in_dim(g, zl * rows, rows, 1)
    swapped = lax.ppermute(lax.dynamic_slice_in_dim(g, (1 - zl) * rows, rows, 1), "zl", [(0, 1), (1, 0)])
    a = lax.all_gather(x[:, :FIRST], ("zh", "zl"), axis=0, tiled=True)
    b = lax.optimization_barrier((x, swapped))[0][:, FIRST:]

    pair = jnp.stack([mine, swapped])
    first, last = along(pair, "y", 1), along(pair, "y", -1)
    own = jnp.stack([pair, first, along(first, "y", 1), last])
    b = lax.all_gather(lax.optimization_barrier((b, a, own))[0], ("zh", "zl"), axis=0, tiled=True)
    theirs = other_core(own)

    places, starts = [], []
    for s in range(8):
        owner = (z - s + 8) % 8
        index = (way * (y - owner // 2) + 8) % 4
        places += [index, (4 - index) % 4]
        starts += [owner * tok + c * half, owner * tok + (1 - c) * half]
    blocks = [(me + way * d + 4) % 4 for d in (2, 1, -1, 0)]
    where = jnp.stack([*places, *starts, *blocks]).astype(jnp.int32)

    def summed(x_all):
        (far,) = product(where, own, theirs, x_all, (0,))
        through = along(far, "x", 1)
        ahead, behind = product(where, own, theirs, x_all, (1, 2))
        up, down = along(ahead + through, "x", 1), along(behind, "x", -1)
        (out,) = product(where, own, theirs, x_all, (3,))
        return (out + up + down).astype(jnp.bfloat16)

    out_a = summed(a)
    out_b = summed(lax.optimization_barrier((b, out_a))[0])
    return jnp.concatenate([out_a, out_b], 1)


def solution(mesh):
    devices = mesh.devices.reshape(4, 4, 2, 2, 4)
    return jax.shard_map(
        body,
        mesh=Mesh(devices, ("zh", "y", "c", "zl", "x")),
        in_specs=(P(("zl", "x"), ("y", "c"), "zh"), P(("zl", "x"), "zh", ("y", "c"))),
        out_specs=P(("zh", "zl", "x"), ("y", "c")),
        check_vma=False,
    )
```

```python
import functools

import jax
import jax.numpy as jnp
from jax import lax
from jax.experimental import pallas as pl
from jax.experimental.pallas import tpu as pltpu
from jax.sharding import Mesh, PartitionSpec as P

FIRST = 640


def along(x, axis, way):
    inner = axis == "x"
    at = lambda i, c: c * 4 + i if inner else i * 2 + c
    pairs = [(at(i, c), at((i + (way if c == 0 else -way)) % 4, c)) for i in range(4) for c in range(2)]
    return lax.ppermute(x, ("c", "x") if inner else ("y", "c"), pairs)


def other_core(x):
    return lax.ppermute(x, "c", [(0, 1), (1, 0)])


def product_kernel(where, *refs):
    grads, x_ref, outs = refs[:16], refs[16], refs[17:]
    half = grads[0].shape[0]
    total = None
    for k, grad in enumerate(grads):
        tokens = x_ref[pl.ds(pl.multiple_of(where[16 + k], half), half), :]
        term = lax.dot_general(grad[...], tokens, (((0,), (0,)), ((), ())), preferred_element_type=jnp.float32)
        total = term if total is None else total + term
    for step, out in enumerate(outs):
        pl.when(pl.program_id(0) == step)(functools.partial(out.__setitem__, ..., total))


def product(where, own, theirs, x, blocks):
    half, rows = own.shape[2:]
    width, block = x.shape[1], rows // 4

    def grad_block(k):
        return pl.BlockSpec((None, None, half, block), lambda i, where: (where[k], k // 2 % 2, 0, where[32 + blocks[0] + i]))

    out = jax.ShapeDtypeStruct((block, width), jnp.float32)
    return pl.pallas_call(
        product_kernel,
        grid_spec=pltpu.PrefetchScalarGridSpec(
            num_scalar_prefetch=1,
            grid=(len(blocks),),
            in_specs=[*map(grad_block, range(16)), pl.BlockSpec(x.shape, lambda i, where: (0, 0))],
            out_specs=[pl.BlockSpec((block, width), lambda i, where: (0, 0))] * len(blocks),
        ),
        out_shape=[out] * len(blocks),
        compiler_params=pltpu.CompilerParams(vmem_limit_bytes=22 * 2**20),
        cost_estimate=pl.CostEstimate(
            flops=2 * x.size * block * len(blocks),
            bytes_accessed=2 * x.size + (2 * x.shape[0] + 4 * width) * block * len(blocks),
            transcendentals=0,
        ),
    )(where, *([own, theirs] * 8), x)


def body(grad_out, inputs):
    g, x = grad_out[0], inputs[0]
    zh, zl, y, me, c = (lax.axis_index(name) for name in ("zh", "zl", "y", "x", "c"))
    way = 1 - 2 * c
    z = zh * 2 + zl
    rows, tok = g.shape[1] // 2, x.shape[0]
    half, block = tok // 2, rows // 4
    mine = lax.dynamic_slice_in_dim(g, zl * rows, rows, 1)
    swapped = lax.ppermute(lax.dynamic_slice_in_dim(g, (1 - zl) * rows, rows, 1), "zl", [(0, 1), (1, 0)])
    a = lax.all_gather(x[:, :FIRST], ("zh", "zl"), axis=0, tiled=True)
    b = lax.optimization_barrier((x, swapped))[0][:, FIRST:]

    pair = jnp.stack([mine, swapped])
    first, last = along(pair, "y", 1), along(pair, "y", -1)
    own = jnp.stack([pair, first, along(first, "y", 1), last])
    b = lax.all_gather(lax.optimization_barrier((b, a, own))[0], ("zh", "zl"), axis=0, tiled=True)
    theirs = other_core(own)

    places, starts = [], []
    for s in range(8):
        owner = (z - s + 8) % 8
        index = (way * (y - owner // 2) + 8) % 4
        places += [index, (4 - index) % 4]
        starts += [owner * tok + c * half, owner * tok + (1 - c) * half]
    blocks = [(me + way * d + 4) % 4 for d in (2, -1, 1, 0)]
    where = jnp.stack([*places, *starts, *blocks]).astype(jnp.int32)

    def summed(x_all):
        far, behind = product(where, own, theirs, x_all, (0, 1))
        through, down = along(far, "x", 1), along(behind, "x", -1)
        (ahead,) = product(where, own, theirs, x_all, (2,))
        up = along(ahead + through, "x", 1)
        (out,) = product(where, own, theirs, x_all, (3,))
        return (out + up + down).astype(jnp.bfloat16)

    out_a = summed(a)
    out_b = summed(lax.optimization_barrier((b, out_a))[0])
    return jnp.concatenate([out_a, out_b], 1)


def solution(mesh):
    devices = mesh.devices.reshape(4, 4, 2, 2, 4)
    return jax.shard_map(
        body,
        mesh=Mesh(devices, ("zh", "y", "c", "zl", "x")),
        in_specs=(P(("zl", "x"), ("y", "c"), "zh"), P(("zl", "x"), "zh", ("y", "c"))),
        out_specs=P(("zh", "zl", "x"), ("y", "c")),
        check_vma=False,
    )
```

```python
import functools

import jax
import jax.numpy as jnp
from jax import lax
from jax.experimental import pallas as pl
from jax.experimental.pallas import tpu as pltpu
from jax.sharding import Mesh, PartitionSpec as P

FIRST = 640


def along(x, axis, way):
    inner = axis == "x"
    at = lambda i, c: c * 4 + i if inner else i * 2 + c
    pairs = [(at(i, c), at((i + (way if c == 0 else -way)) % 4, c)) for i in range(4) for c in range(2)]
    return lax.ppermute(x, ("c", "x") if inner else ("y", "c"), pairs)


def other_core(x):
    return lax.ppermute(x, "c", [(0, 1), (1, 0)])


def product_kernel(where, *refs):
    grads, x_ref, outs = refs[:16], refs[16], refs[17:]
    half = grads[0].shape[0]
    total = None
    for k, grad in enumerate(grads):
        tokens = x_ref[pl.ds(pl.multiple_of(where[16 + k], half), half), :]
        term = lax.dot_general(grad[...], tokens, (((0,), (0,)), ((), ())), preferred_element_type=jnp.float32)
        total = term if total is None else total + term
    for step, out in enumerate(outs):
        pl.when(pl.program_id(0) == step)(functools.partial(out.__setitem__, ..., total))


def product(where, own, theirs, x, blocks):
    half, rows = own.shape[2:]
    width, block = x.shape[1], rows // 4

    def grad_block(k):
        return pl.BlockSpec((None, None, half, block), lambda i, where: (where[k], k // 2 % 2, 0, where[32 + blocks[0] + i]))

    out = jax.ShapeDtypeStruct((block, width), jnp.float32)
    return pl.pallas_call(
        product_kernel,
        grid_spec=pltpu.PrefetchScalarGridSpec(
            num_scalar_prefetch=1,
            grid=(len(blocks),),
            in_specs=[*map(grad_block, range(16)), pl.BlockSpec(x.shape, lambda i, where: (0, 0))],
            out_specs=[pl.BlockSpec((block, width), lambda i, where: (0, 0))] * len(blocks),
        ),
        out_shape=[out] * len(blocks),
        compiler_params=pltpu.CompilerParams(vmem_limit_bytes=22 * 2**20),
        cost_estimate=pl.CostEstimate(
            flops=2 * x.size * block * len(blocks),
            bytes_accessed=2 * x.size + (2 * x.shape[0] + 4 * width) * block * len(blocks),
            transcendentals=0,
        ),
    )(where, *([own, theirs] * 8), x)


def body(grad_out, inputs):
    g, x = grad_out[0], inputs[0]
    zh, zl, y, me, c = (lax.axis_index(name) for name in ("zh", "zl", "y", "x", "c"))
    way = 1 - 2 * c
    z = zh * 2 + zl
    rows, tok = g.shape[1] // 2, x.shape[0]
    half, block = tok // 2, rows // 4
    mine = lax.dynamic_slice_in_dim(g, zl * rows, rows, 1)
    swapped = lax.ppermute(lax.dynamic_slice_in_dim(g, (1 - zl) * rows, rows, 1), "zl", [(0, 1), (1, 0)])
    a = lax.all_gather(x[:, :FIRST], ("zh", "zl"), axis=0, tiled=True)
    b = lax.optimization_barrier((x, swapped))[0][:, FIRST:]

    pair = jnp.stack([mine, swapped])
    first, last = along(pair, "y", 1), along(pair, "y", -1)
    own = jnp.stack([pair, first, along(first, "y", 1), last])
    b = lax.all_gather(lax.optimization_barrier((b, own))[0], ("zh", "zl"), axis=0, tiled=True)
    theirs = other_core(own)

    places, starts = [], []
    for s in range(8):
        owner = (z - s + 8) % 8
        index = (way * (y - owner // 2) + 8) % 4
        places += [index, (4 - index) % 4]
        starts += [owner * tok + c * half, owner * tok + (1 - c) * half]
    blocks = [(me + way * d + 4) % 4 for d in (2, 1, -1, 0)]
    where = jnp.stack([*places, *starts, *blocks]).astype(jnp.int32)

    def summed(x_all):
        (far,) = product(where, own, theirs, x_all, (0,))
        through = along(far, "x", 1)
        ahead, behind = product(where, own, theirs, x_all, (1, 2))
        up, down = along(ahead + through, "x", 1), along(behind, "x", -1)
        (out,) = product(where, own, theirs, x_all, (3,))
        return (out + up + down).astype(jnp.bfloat16)

    out_a = summed(a)
    out_b = summed(lax.optimization_barrier((b, out_a))[0])
    return jnp.concatenate([out_a, out_b], 1)


def solution(mesh):
    devices = mesh.devices.reshape(4, 4, 2, 2, 4)
    return jax.shard_map(
        body,
        mesh=Mesh(devices, ("zh", "y", "c", "zl", "x")),
        in_specs=(P(("zl", "x"), ("y", "c"), "zh"), P(("zl", "x"), "zh", ("y", "c"))),
        out_specs=P(("zh", "zl", "x"), ("y", "c")),
        check_vma=False,
    )
```
